512 devices in a mesh: replica: 16 (over z_hi, x), tensor: 32 (over y, z_lo, core).
Axes of the slice: x: 4, y: 4, z: 16 (z_hi: 4, z_lo: 4; z = z_hi * 4 + z_lo), core: 2. Of those that a mesh axis runs over, the one named last changes fastest.
Arguments:
- attn_out: bfloat16 [16, 1024, 4096], P('replica', None, 'tensor'), may hold values from -6 to 6
- resid_in: bfloat16 [16, 1024, 2048], P('replica', 'tensor')
- out_weight: bfloat16 [16, 4096, 2048], P('replica', 'tensor'), may hold values from -6 to 6
- velocity: bfloat16 [16, 4096, 2048], P('replica', 'tensor'), may hold values from -6 to 6
- norm_gain: bfloat16 [2048], replicated, may hold values from 0.099609375 to 1.8984375
- grad_normed: bfloat16 [16, 1024, 2048], P('replica', 'tensor'), may hold values from -6 to 6
- grad_resid: bfloat16 [16, 1024, 2048], P('replica', 'tensor'), may hold values from -6 to 6
- step_count: int32 [1], replicated, may hold values from 0 to 1048575
Outputs:
- stream: bfloat16 [16, 1024, 2048], P('replica', 'tensor')
- grad_attn: bfloat16 [16, 1024, 4096], P('replica', None, 'tensor')
- new_weight: bfloat16 [16, 4096, 2048], P('replica', 'tensor')
- new_velocity: bfloat16 [16, 4096, 2048], P('replica', 'tensor')
The draws below stay inside these ranges and needn't reach their ends.
All inputs are finite; a program needn't handle non-finite values.
Results may differ from the reference program's by a relative error of at most 0.015.
Values may be sent and summed in bfloat16 or wider, within the bound.
A program may use at most 64 MiB of HBM per device.

```python
import math
import jax
import jax.numpy as jnp
from jax import lax

D = 2048
TOK = 1024
INNER = 4096
REPLICAS = 16
N_REPLICA = 16
N_TENSOR = 32


def draw_resid_in(key, part):
    key = jax.random.fold_in(key, 7)
    key_base, key_rows, key_cols = jax.random.split(key, 3)
    base = jax.random.normal(key_base, (REPLICAS, TOK, D), jnp.float32)
    row_scale = jnp.exp(jax.random.uniform(key_rows, (REPLICAS, TOK, 1), jnp.float32, math.log(0.3), math.log(3.0)))
    col_scale = jnp.exp(jax.random.uniform(key_cols, (1, 1, D), jnp.float32, math.log(0.3), math.log(3.0)))
    return (base * row_scale * col_scale).astype(jnp.bfloat16)


def level_of(stream_key, extent, pieces, least, largest):
    gain = 1.0
    for axis_at, blocks in pieces:
        heights = jax.random.uniform(jax.random.fold_in(jax.random.fold_in(stream_key, 6), axis_at), (blocks,), jnp.float32, least / len(pieces), largest / len(pieces))
        gain = gain * jnp.repeat(jnp.exp(heights), extent[axis_at] // blocks).reshape((-1,) + (1,) * (len(extent) - 1 - axis_at))
    return gain


def noise(own_key, dims, spread, limit, cuts=(), kind=jnp.bfloat16):
    entries = jax.random.normal(own_key, dims, jnp.float32) * spread
    if len(cuts) > 0:
        entries = level_of(own_key, dims, cuts, -0.22, 0.18) * entries
    return jnp.clip(entries, min=-limit, max=limit).astype(kind)


def setup_inputs(seed: int = 0) -> dict:
    keys = jax.random.split(jax.random.key(seed), 9)
    attn_out = noise(keys[0], (REPLICAS, TOK, INNER), 1.0, 6.0, ((0, 16), (2, 32)))
    resid_in = draw_resid_in(jax.random.fold_in(keys[8], 71), 0)
    out_weight = noise(keys[2], (REPLICAS, INNER, D), 1.0, 6.0, ((0, 16), (1, 32)))
    velocity = noise(keys[3], (REPLICAS, INNER, D), 1.0, 6.0, ((0, 16), (1, 32)))
    norm_gain = jnp.clip(1.0 + 0.18 * jax.random.normal(keys[4], (D,), jnp.float32), 0.099609375, 1.8984375).astype(jnp.bfloat16)
    grad_normed = noise(keys[5], (REPLICAS, TOK, D), 1.0, 6.0, ((0, 16), (1, 32)))
    grad_resid = noise(keys[6], (REPLICAS, TOK, D), 1.0, 6.0, ((0, 16), (1, 32)))
    step_count = jax.random.randint(keys[7], (1,), 0, 1048576).astype(jnp.int32)
    return {"attn_out": attn_out, "resid_in": resid_in, "out_weight": out_weight, "velocity": velocity, "norm_gain": norm_gain, "grad_normed": grad_normed, "grad_resid": grad_resid, "step_count": step_count}


norm_eps = 1e-05
decay_coef = 0.9
step_span = 1048576.0

def plan_rate(step_value):
    phase = step_value.astype(jnp.float32) * (jnp.pi / step_span)
    return 0.02 + 0.04 * (1.0 + jnp.cos(phase))

def replica_pass(heads_out, resid_rows, weight, norm_gain, grad_norm_rows, grad_resid_rows):
    inv_width = INNER ** (-0.5)
    group_cols = INNER // N_TENSOR
    grouped = heads_out.reshape(TOK, N_TENSOR, group_cols).transpose(1, 0, 2)
    weight_groups = weight.reshape(N_TENSOR, group_cols, D)

    def add_group(total, members):
        product = (jnp.dot(members[0], members[1], preferred_element_type=jnp.float32) * inv_width).astype(jnp.bfloat16)
        product = lax.optimization_barrier(product)
        return (total + product.astype(jnp.float32), None)
    projected, _ = lax.scan(add_group, jnp.zeros((TOK, D), jnp.float32), (grouped, weight_groups))
    stream = (resid_rows.astype(jnp.float32) + projected).astype(jnp.bfloat16)
    stream32 = stream.astype(jnp.float32)
    inv_rms = lax.rsqrt(lax.optimization_barrier(jnp.mean(stream32 * stream32, axis=-1, keepdims=True)) + norm_eps)
    upstream = norm_gain.astype(jnp.float32) * grad_norm_rows.astype(jnp.float32)
    inner_sum = lax.optimization_barrier(jnp.sum(upstream * stream32, axis=-1, keepdims=True))
    dstream = grad_resid_rows.astype(jnp.float32) + inv_rms * upstream - stream32 * inv_rms ** 3 * inner_sum / D
    dstream = dstream.astype(jnp.bfloat16)
    weight_grad = (jnp.dot(heads_out.T, dstream, preferred_element_type=jnp.float32) * inv_width).astype(jnp.bfloat16)
    input_grad = (jnp.dot(dstream, weight.T, preferred_element_type=jnp.float32) * inv_width).astype(jnp.bfloat16)
    return (stream, input_grad, weight_grad)

def reference(attn_out, resid_in, out_weight, velocity, norm_gain, grad_normed, grad_resid, step_count):

    def one_replica(members):
        return replica_pass(members[0], members[1], members[2], norm_gain, members[3], members[4])
    stream, grad_attn, weight_grad = lax.map(one_replica, (attn_out, resid_in, out_weight, grad_normed, grad_resid))
    bit_count = N_REPLICA.bit_length() - 1
    peer_bit = step_count[0] % bit_count
    learn_rate = plan_rate(step_count[0])
    indices = jnp.arange(N_REPLICA, dtype=jnp.int32)
    peers = jnp.bitwise_xor(indices, jnp.left_shift(jnp.int32(1), peer_bit.astype(jnp.int32)))

    def mix(replica_index):
        other = peers[replica_index]
        own_velocity = velocity[replica_index].astype(jnp.float32)
        peer_velocity = velocity[other].astype(jnp.float32)
        own_grad = weight_grad[replica_index].astype(jnp.float32)
        peer_grad = weight_grad[other].astype(jnp.float32)
        mixed_velocity = decay_coef * 0.5 * (own_velocity + peer_velocity) + 0.5 * (own_grad + peer_grad)
        mean_weight = 0.5 * (out_weight[replica_index].astype(jnp.float32) + out_weight[other].astype(jnp.float32))
        return ((mean_weight - learn_rate * mixed_velocity).astype(jnp.bfloat16), mixed_velocity.astype(jnp.bfloat16))
    new_weight, new_velocity = lax.map(mix, indices)
    return (stream, grad_attn, new_weight, new_velocity)
```

```python
from functools import partial

import jax
import jax.numpy as jnp
from jax import lax
from jax.experimental import pallas as pl
from jax.experimental.pallas import tpu as pltpu
from jax.sharding import PartitionSpec as P

D = 2048
INNER = 4096
TOK = 1024
GROUP = 128
CHUNKS = 4
WIDE = D // CHUNKS
BF16 = jnp.bfloat16
F32 = jnp.float32
MESH = pl.DeviceIdType.MESH

norm_eps = 1e-05
decay_coef = 0.9
step_span = 1048576.0
inv_width = INNER ** (-0.5)


def plan_rate(step_value):
    phase = step_value.astype(jnp.float32) * (jnp.pi / step_span)
    return 0.02 + 0.04 * (1.0 + jnp.cos(phase))


def flip(digit, mask):
    if mask == 1:
        return digit + 1 - 2 * (digit % 2)
    if mask == 2:
        return (digit + 2) % 4
    return 3 - digit


def cols(k):
    return pl.ds(k * WIDE, WIDE)


def kernel(
    bit,
    attn, resid, weight, velocity, gain, grad_normed, grad_resid, rate,
    stream_out, grad_attn_out, new_weight_out, new_velocity_out,
    acat, wcat, acat_t, s1, r1, keep, s2, r2, s3, r3, full,
    resid_v, gn_v, gr_v, up_v, stream_v, vel_v,
    ga, ga_send, ga_own, g_own, g_send, g_recv, vloc, v_send, v_hop, v_recv, w_hop, w_recv,
    nw_v, nv_v, local_sem, send_sem, recv_sem,
):
    me_r = lax.axis_index("replica")
    me_t = lax.axis_index("tensor")
    y, z, c = me_t // 8, (me_t // 2) % 4, me_t % 2
    relay = bit % 2 == 1

    def at(y_, z_, c_):
        return (me_r, (y_ * 4 + z_) * 2 + c_)

    def peer_at(mask):
        if bit < 2:
            return (me_r - me_r % 4 + flip(me_r % 4, mask), me_t)
        return (flip(me_r // 4, mask) * 4 + me_r % 4, me_t)

    sibling = at(y, z, 1 - c)
    y1, y3 = at(flip(y, 1), z, c), at(flip(y, 3), z, c)
    z_at = [at(y, flip(z, j), c) for j in (1, 2, 3)]
    if relay:
        one, three = peer_at(1)[0], peer_at(3)[0]
        hop1 = (one * (1 - c) + three * c, me_t)
        hop2 = (three * (1 - c) + one * c, me_t)
        peers = [hop1, hop2]
    else:
        hop1 = hop2 = peer_at(1)
        peers = [hop2]

    slots = [0]

    def remote(src, dst, target):
        slot = slots[0]
        slots[0] += 1
        return pltpu.make_async_remote_copy(
            src_ref=src, dst_ref=dst, send_sem=send_sem.at[slot], recv_sem=recv_sem.at[slot],
            device_id=target, device_id_type=MESH,
        )

    local_slots = [0]

    def local(src, dst):
        slot = local_slots[0]
        local_slots[0] += 1
        copy = pltpu.make_async_copy(src, dst, local_sem.at[slot])
        copy.start()
        return copy

    barrier = pltpu.get_barrier_semaphore()
    partners = [sibling, y1, y3] + z_at + peers
    for partner in partners:
        pl.semaphore_signal(barrier, inc=1, device_id=partner, device_id_type=MESH)

    in_a = local(attn.at[:, c], acat.at[:, :, pl.ds(0, GROUP)])
    in_w = local(weight, wcat.at[pl.ds(0, GROUP)])
    in_rest = [
        local(resid, resid_v), local(grad_normed, gn_v),
        local(grad_resid, gr_v), local(velocity, vel_v),
    ]
    pl.semaphore_wait(barrier, len(partners))

    sends = []

    def go(copy):
        copy.start()
        sends.append(copy)
        return copy

    sib_a = go(remote(attn.at[:, 1 - c], acat.at[:, :, pl.ds(GROUP, GROUP)], sibling))
    sib_w = go(remote(weight, wcat.at[pl.ds(GROUP, GROUP)], sibling))
    if relay:
        w_first = go(remote(weight, w_hop, hop1))
        w_last = remote(w_hop, w_recv, hop2)
    else:
        w_last = go(remote(weight, w_recv, hop2))

    in_a.wait()
    in_w.wait()
    sib_a.wait_recv()
    sib_w.wait_recv()

    def rows_for(dest):
        return acat[pl.ds(dest * 4, 4)].reshape(128, 2 * GROUP)

    def product(dest, k):
        return (
            jnp.dot(rows_for(dest), wcat[:, cols(k)], preferred_element_type=F32) * inv_width
        )

    first = [1 if k % 2 == 0 else 3 for k in range(CHUNKS)]
    second = [3 if k % 2 == 0 else 1 for k in range(CHUNKS)]
    along_y = {1: y1, 3: y3}

    step1 = []
    for k in range(CHUNKS):
        s1[k, 0] = product(flip(y, first[k]), k).astype(BF16)
        s1[k, 1] = product(flip(y, 2), k).astype(BF16)
        step1.append(go(remote(s1.at[k], r1.at[k], along_y[first[k]])))
    for k in range(CHUNKS):
        keep[k, 1] = product(flip(y, second[k]), k)
        keep[k, 0] = product(y, k)
    for copy in in_rest:
        copy.wait()
    up_v[...] = gain[...].astype(F32) * gn_v[...].astype(F32)
    acat_t[...] = acat[...].reshape(512, 2 * GROUP).T

    step2 = []
    for k in range(CHUNKS):
        step1[k].wait_recv()
        s2[k] = (keep[k, 1] + r1[k, 1].astype(F32)).astype(BF16)
        step2.append(go(remote(s2.at[k], r2.at[k], along_y[second[k]])))
    step3 = []
    for k in range(CHUNKS):
        step2[k].wait_recv()
        total = keep[k, 0] + r1[k, 0].astype(F32) + r2[k].astype(F32)
        s3[k] = total.astype(BF16).reshape(4, 32, WIDE)
        step3.append([
            go(remote(s3.at[k, flip(z, j)], r3.at[k, j - 1], z_at[j - 1])) for j in (1, 2, 3)
        ])
    squares = jnp.zeros((32, 1), F32)
    inner = jnp.zeros((32, 1), F32)
    for k in range(CHUNKS):
        projected = s3[k, z].astype(F32)
        for j in (1, 2, 3):
            step3[k][j - 1].wait_recv()
            projected += r3[k, j - 1].astype(F32)
        stream = (resid_v[:, cols(k)].astype(F32) + projected).astype(BF16)
        stream_v[:, cols(k)] = stream
        stream32 = stream.astype(F32)
        squares += jnp.sum(stream32 * stream32, axis=-1, keepdims=True)
        inner += jnp.sum(up_v[:, cols(k)] * stream32, axis=-1, keepdims=True)
    out_copies = [local(stream_v, stream_out)]
    inv_rms = lax.rsqrt(squares / D + norm_eps)
    factor = inv_rms * inv_rms * inv_rms * inner / D

    own = y * 4 + z
    gz = []
    for k in range(CHUNKS):
        d = (
            gr_v[:, cols(k)].astype(F32)
            + inv_rms * up_v[:, cols(k)]
            - stream_v[:, cols(k)].astype(F32) * factor
        )
        full[k, own] = d.astype(BF16)
        gz.append([go(remote(full.at[k, own], full.at[k, own], z_at[j - 1])) for j in (1, 2, 3)])
    if relay:
        w_first.wait_recv()
        go(w_last)
    gy = []
    for k in range(CHUNKS):
        for copy in gz[k]:
            copy.wait_recv()
        block = full.at[k, pl.ds(y * 4, 4)]
        gy.append({m: go(remote(block, block, along_y[m])) for m in (1, 3)})
    gf = []
    for k in range(CHUNKS):
        gy[k][first[k]].wait_recv()
        block = full.at[k, pl.ds(flip(y, first[k]) * 4, 4)]
        gf.append(go(remote(block, block, along_y[second[k]])))

    v_first, v_last, g_swap = [], [], []

    def finish_velocity(k):
        g_swap[k].wait_recv()
        grad = ((g_own[k] + g_recv[k].astype(F32)) * inv_width).astype(BF16)
        mine = decay_coef * vel_v[:, cols(k)].astype(F32) + grad.astype(F32)
        vloc[k] = mine
        v_send[k] = mine.astype(BF16)
        if relay:
            v_first.append(go(remote(v_send.at[k], v_hop.at[k], hop1)))
        else:
            v_last.append(go(remote(v_send.at[k], v_recv.at[k], hop2)))

    for k in range(CHUNKS):
        gy[k][second[k]].wait_recv()
        gf[k].wait_recv()
        rows = full[k].reshape(512, WIDE)
        both = jnp.dot(acat_t[...], rows, preferred_element_type=F32)
        g_send[k] = both[GROUP:].astype(BF16)
        g_own[k] = both[:GROUP]
        g_swap.append(go(remote(g_send.at[k], g_recv.at[k], sibling)))
        part = lax.dot_general(
            rows, wcat[:, cols(k)], (((1,), (1,)), ((), ())), preferred_element_type=F32
        )
        ga[...] = part if k == 0 else ga[...] + part
        if k > 0:
            finish_velocity(k - 1)
    finish_velocity(CHUNKS - 1)
    ga_send[...] = (ga[:, GROUP:] * inv_width).astype(BF16).reshape(16, 32, GROUP)
    ga_swap = go(remote(ga_send, grad_attn_out.at[:, c], sibling))
    ga_own[...] = (ga[:, :GROUP] * inv_width).astype(BF16).reshape(16, 32, GROUP)
    out_copies.append(local(ga_own, grad_attn_out.at[:, c]))

    if relay:
        for k in range(CHUNKS):
            v_first[k].wait_recv()
            v_last.append(go(remote(v_hop.at[k], v_recv.at[k], hop2)))
    w_last.wait_recv()
    for k in range(CHUNKS):
        v_last[k].wait_recv()
        mixed = 0.5 * (vloc[k] + v_recv[k].astype(F32))
        nv_v[:, cols(k)] = mixed.astype(BF16)
        mean = 0.5 * (wcat[:GROUP, cols(k)].astype(F32) + w_recv[:, cols(k)].astype(F32))
        nw_v[:, cols(k)] = (mean - rate[0] * mixed).astype(BF16)
        out_copies.append(local(nv_v.at[:, cols(k)], new_velocity_out.at[:, cols(k)]))
        out_copies.append(local(nw_v.at[:, cols(k)], new_weight_out.at[:, cols(k)]))
    ga_swap.wait_recv()
    for copy in out_copies:
        copy.wait()
    for copy in sends:
        copy.wait_send()


def step_with(bit, *operands):
    any_spec = pl.BlockSpec(memory_space=pl.ANY)
    vmem = lambda *shape: pltpu.VMEM(shape, BF16)
    wide = lambda *shape: pltpu.VMEM(shape, F32)
    remote_slots = 2 + 2 + CHUNKS * (1 + 1 + 3 + 3 + 2 + 1 + 1 + 2) + 1
    return pl.pallas_call(
        partial(kernel, bit),
        out_shape=(
            jax.ShapeDtypeStruct((32, D), BF16),
            jax.ShapeDtypeStruct((16, 2, 32, GROUP), BF16),
            jax.ShapeDtypeStruct((GROUP, D), BF16),
            jax.ShapeDtypeStruct((GROUP, D), BF16),
        ),
        in_specs=[any_spec] * 4
        + [pl.BlockSpec(memory_space=pltpu.VMEM)]
        + [any_spec] * 2
        + [pl.BlockSpec(memory_space=pltpu.SMEM)],
        out_specs=(any_spec,) * 4,
        scratch_shapes=[
            vmem(16, 32, 2 * GROUP),
            vmem(2 * GROUP, D),
            vmem(2 * GROUP, 512),
            vmem(CHUNKS, 2, 128, WIDE),
            vmem(CHUNKS, 2, 128, WIDE),
            wide(CHUNKS, 2, 128, WIDE),
            vmem(CHUNKS, 128, WIDE),
            vmem(CHUNKS, 128, WIDE),
            vmem(CHUNKS, 4, 32, WIDE),
            vmem(CHUNKS, 3, 32, WIDE),
            vmem(CHUNKS, 16, 32, WIDE),
            vmem(32, D),
            vmem(32, D),
            vmem(32, D),
            wide(32, D),
            vmem(32, D),
            vmem(GROUP, D),
            wide(512, 2 * GROUP),
            vmem(16, 32, GROUP),
            vmem(16, 32, GROUP),
            wide(CHUNKS, GROUP, WIDE),
            vmem(CHUNKS, GROUP, WIDE),
            vmem(CHUNKS, GROUP, WIDE),
            wide(CHUNKS, GROUP, WIDE),
            vmem(CHUNKS, GROUP, WIDE),
            vmem(CHUNKS, GROUP, WIDE),
            vmem(CHUNKS, GROUP, WIDE),
            vmem(GROUP, D),
            vmem(GROUP, D),
            vmem(GROUP, D),
            vmem(GROUP, D),
            pltpu.SemaphoreType.DMA((6 + 2 + 2 * CHUNKS,)),
            pltpu.SemaphoreType.DMA((remote_slots,)),
            pltpu.SemaphoreType.DMA((remote_slots,)),
        ],
        compiler_params=pltpu.CompilerParams(
            collective_id=bit, has_side_effects=True, vmem_limit_bytes=48 * 1024 * 1024
        ),
        cost_estimate=pl.CostEstimate(
            flops=6 * TOK * GROUP * D, bytes_accessed=8 * 1024 * 1024, transcendentals=64
        ),
        name="step_bit%d" % bit,
    )(*operands)


def per_device(
    attn_out, resid_in, out_weight, velocity, norm_gain, grad_normed, grad_resid, step_count
):
    peer_bit = step_count[0] % 4
    rate = plan_rate(step_count)
    stream, grad_attn, new_weight, new_velocity = lax.switch(
        peer_bit,
        [partial(step_with, bit) for bit in range(4)],
        attn_out.reshape(16, 2, 32, GROUP),
        resid_in[0],
        out_weight[0],
        velocity[0],
        norm_gain.reshape(1, D),
        grad_normed[0],
        grad_resid[0],
        rate,
    )
    return (
        stream[None],
        grad_attn.reshape(1, TOK, GROUP),
        new_weight[None],
        new_velocity[None],
    )


def solution(mesh):
    rows = P("replica", "tensor", None)
    heads = P("replica", None, "tensor")
    return jax.shard_map(
        per_device,
        mesh=mesh,
        in_specs=(heads, rows, rows, rows, P(), rows, rows, P()),
        out_specs=(rows, heads, rows, rows),
        check_vma=False,
    )
```

```python
from functools import partial

import jax
import jax.numpy as jnp
from jax import lax
from jax.experimental import pallas as pl
from jax.experimental.pallas import tpu as pltpu
from jax.sharding import PartitionSpec as P

D = 2048
INNER = 4096
TOK = 1024
GROUP = 128
CHUNKS = 4
WIDE = D // CHUNKS
AHEAD = CHUNKS // 2
QUARTER = CHUNKS // 4
PIECES = 8
ONLY = ((0,) * 8, (0, 1, 2, 3, 4, 5, 6, 7))
FIRST = ((0,) * 8, (0, 0, 2, 2, 4, 4, 6, 6))
LAST = ((3,) * 8, (8,) * 8)
BF16 = jnp.bfloat16
F32 = jnp.float32
MESH = pl.DeviceIdType.MESH

norm_eps = 1e-05
decay_coef = 0.9
step_span = 1048576.0
inv_width = INNER ** (-0.5)


def plan_rate(step_value):
    phase = step_value.astype(jnp.float32) * (jnp.pi / step_span)
    return 0.02 + 0.04 * (1.0 + jnp.cos(phase))


def flip(digit, mask):
    if mask == 1:
        return digit + 1 - 2 * (digit % 2)
    if mask == 2:
        return (digit + 2) % 4
    return 3 - digit


def cols(k):
    return pl.ds(k * WIDE, WIDE)


def kernel(
    bit,
    attn, resid, weight, velocity, gain, grad_normed, grad_resid, rate,
    stream_out, grad_attn_out, new_weight_out, new_velocity_out,
    acat, wcat, acat_t, s1, r1, keep, s2, r2, s3, r3, full,
    resid_v, gain_v, gn_v, gr_v, up_v, stream_v, vel_v,
    ga, ga_send, ga_own, g_own, g_send, g_recv, vloc, v_send, v_hop, v_recv, w_hop, w_recv,
    nw_v, nv_v, local_sem, send_sem, recv_sem,
):
    me_r = lax.axis_index("replica")
    me_t = lax.axis_index("tensor")
    y, z, c = me_t // 8, (me_t // 2) % 4, me_t % 2
    relay = bit % 2 == 1

    def at(y_, z_, c_):
        return (me_r, (y_ * 4 + z_) * 2 + c_)

    def peer_at(mask):
        if bit < 2:
            return (me_r - me_r % 4 + flip(me_r % 4, mask), me_t)
        return (flip(me_r // 4, mask) * 4 + me_r % 4, me_t)

    sibling = at(y, z, 1 - c)
    y1, y3 = at(flip(y, 1), z, c), at(flip(y, 3), z, c)
    z_at = [at(y, flip(z, j), c) for j in (1, 2, 3)]
    if relay:
        one, three = peer_at(1)[0], peer_at(3)[0]
        hop1 = (one * (1 - c) + three * c, me_t)
        hop2 = (three * (1 - c) + one * c, me_t)
        peers = [hop1, hop2]
    else:
        hop1 = hop2 = peer_at(1)
        peers = [hop2]

    slots = [0]

    def remote(src, dst, target):
        slot = slots[0]
        slots[0] += 1
        return pltpu.make_async_remote_copy(
            src_ref=src, dst_ref=dst, send_sem=send_sem.at[slot], recv_sem=recv_sem.at[slot],
            device_id=target, device_id_type=MESH,
        )

    local_slots = [0]

    def local(src, dst):
        slot = local_slots[0]
        local_slots[0] += 1
        copy = pltpu.make_async_copy(src, dst, local_sem.at[slot])
        copy.start()
        return copy

    barrier = pltpu.get_barrier_semaphore()
    partners = [sibling, y1, y3] + z_at + peers
    for partner in partners:
        pl.semaphore_signal(barrier, inc=1, device_id=partner, device_id_type=MESH)

    in_a = local(attn.at[:, c], acat.at[:, :, pl.ds(0, GROUP)])
    in_w = local(weight, wcat.at[pl.ds(0, GROUP)])
    in_rest = [
        local(resid, resid_v), local(gain, gain_v), local(grad_normed, gn_v),
        local(grad_resid, gr_v), local(velocity, vel_v),
    ]
    pl.semaphore_wait(barrier, len(partners))

    sends = []

    def go(copy):
        copy.start()
        sends.append(copy)
        return copy

    sib_a = go(remote(attn.at[:, 1 - c], acat.at[:, :, pl.ds(GROUP, GROUP)], sibling))
    sib_w = go(remote(weight, wcat.at[pl.ds(GROUP, GROUP)], sibling))
    piece = GROUP // PIECES
    rows = [pl.ds(i * piece, piece) for i in range(PIECES)]
    w_first = [remote(weight.at[r], w_hop.at[r], hop1) for r in rows] if relay else []
    w_last = [
        remote((w_hop if relay else weight).at[r], w_recv.at[r], hop2) for r in rows
    ]
    sends.extend(w_first + w_last)

    def point(i):
        if relay:
            for n in range(PIECES):
                if i == FIRST[bit // 2][n]:
                    w_first[n].start()
                if i == LAST[bit // 2][n]:
                    w_first[n].wait_recv()
                    w_last[n].start()
        else:
            for n in range(PIECES):
                if i == ONLY[bit // 2][n]:
                    w_last[n].start()

    point(0)
    in_a.wait()
    in_w.wait()
    sib_a.wait_recv()
    sib_w.wait_recv()

    def rows_for(dest):
        return acat[pl.ds(dest * 4, 4)].reshape(128, 2 * GROUP)

    along_y = {1: y1, 3: y3}
    first, second = (1, 3), (3, 1)
    half = WIDE // 2

    def part(k, h):
        return pl.ds(k * WIDE + h * half, half)

    def product(dest, k, h):
        return (
            jnp.dot(rows_for(dest), wcat[:, part(k, h)], preferred_element_type=F32) * inv_width
        )

    step1, step2, step3 = {}, {}, {}

    def send1(k):
        for h in (0, 1):
            s1[k, h, 0] = product(flip(y, first[h]), k, h).astype(BF16)
            s1[k, h, 1] = product(flip(y, 2), k, h).astype(BF16)
            step1[k, h] = go(remote(s1.at[k, h], r1.at[k, h], along_y[first[h]]))

    def hold(k):
        for h in (0, 1):
            keep[k, h, 1] = product(flip(y, second[h]), k, h)
            keep[k, h, 0] = product(y, k, h)

    def send2(k):
        for h in (0, 1):
            step1[k, h].wait_recv()
            s2[k, h] = (keep[k, h, 1] + r1[k, h, 1].astype(F32)).astype(BF16)
            step2[k, h] = go(remote(s2.at[k, h], r2.at[k, h], along_y[second[h]]))

    def send3(k):
        for h in (0, 1):
            step2[k, h].wait_recv()
            total = keep[k, h, 0] + r1[k, h, 0].astype(F32) + r2[k, h].astype(F32)
            s3[k, :, :, pl.ds(h * half, half)] = total.astype(BF16).reshape(4, 32, half)
        step3[k] = [
            go(remote(s3.at[k, flip(z, j)], r3.at[k, j - 1], z_at[j - 1])) for j in (1, 2, 3)
        ]

    sums = [jnp.zeros((32, 1), F32), jnp.zeros((32, 1), F32)]

    def add_stream(k):
        projected = s3[k, z].astype(F32)
        for j in (1, 2, 3):
            step3[k][j - 1].wait_recv()
            projected += r3[k, j - 1].astype(F32)
        stream = (resid_v[:, cols(k)].astype(F32) + projected).astype(BF16)
        stream_v[:, cols(k)] = stream
        stream32 = stream.astype(F32)
        sums[0] += jnp.sum(stream32 * stream32, axis=-1, keepdims=True)
        sums[1] += jnp.sum(up_v[:, cols(k)] * stream32, axis=-1, keepdims=True)

    for k in range(AHEAD):
        send1(k)
    for k in range(AHEAD):
        hold(k)
    for k in range(CHUNKS):
        send2(k)
        if k >= 1:
            send3(k - 1)
        if k + AHEAD < CHUNKS:
            send1(k + AHEAD)
            hold(k + AHEAD)
        if k == 1:
            for copy in in_rest:
                copy.wait()
            gain32 = gain_v[...].astype(F32)
            for i in range(D // 128):
                lanes = pl.ds(i * 128, 128)
                up_v[:, lanes] = gain32[i : i + 1] * gn_v[:, lanes].astype(F32)
            acat_t[...] = acat[...].reshape(512, 2 * GROUP).T
        if k >= 2:
            add_stream(k - 2)
        if (k + 1) % QUARTER == 0:
            point((k + 1) // QUARTER)
    send3(CHUNKS - 1)
    add_stream(CHUNKS - 2)
    add_stream(CHUNKS - 1)
    squares, inner = sums
    inv_rms = lax.rsqrt(squares / D + norm_eps)
    factor = inv_rms * inv_rms * inv_rms * inner / D

    own = y * 4 + z
    gz, gy, gf = {}, {}, {}

    def dstream(k):
        d = (
            gr_v[:, cols(k)].astype(F32)
            + inv_rms * up_v[:, cols(k)]
            - stream_v[:, cols(k)].astype(F32) * factor
        )
        full[k, own] = d.astype(BF16)

    def gather_own(k):
        block = full.at[k, own]
        gy[k] = {m: [go(remote(block, block, along_y[m]))] for m in (1, 3)}

    def gather_z(k):
        block = full.at[k, own]
        gz[k] = [go(remote(block, block, z_at[j - 1])) for j in (1, 2, 3)]

    def gather_y(k):
        for j in (1, 2, 3):
            gz[k][j - 1].wait_recv()
            block = full.at[k, y * 4 + flip(z, j)]
            for m in (1, 3):
                gy[k][m].append(go(remote(block, block, along_y[m])))

    def forward_y(k):
        for h in (0, 1):
            for copy in gy[k][first[h]]:
                copy.wait_recv()
            block = full.at[k, pl.ds(flip(y, first[h]) * 4, 4), :, pl.ds(h * half, half)]
            gf[k, h] = go(remote(block, block, along_y[second[h]]))

    v_first, v_last, g_swap = {}, {}, {}

    def weight_part(k):
        gf[k, 0].wait_recv()
        gf[k, 1].wait_recv()
        rows = full[k].reshape(512, WIDE)
        both = jnp.dot(acat_t[...], rows, preferred_element_type=F32)
        g_send[k] = both[GROUP:].astype(BF16)
        g_own[k] = both[:GROUP]
        g_swap[k] = go(remote(g_send.at[k], g_recv.at[k], sibling))

    def attn_part(k):
        rows = full[k].reshape(512, WIDE)
        share = lax.dot_general(
            rows, wcat[:, cols(k)], (((1,), (1,)), ((), ())), preferred_element_type=F32
        )
        ga[...] = share if k == 0 else ga[...] + share

    def send_velocity(k):
        g_swap[k].wait_recv()
        grad = ((g_own[k] + g_recv[k].astype(F32)) * inv_width).astype(BF16)
        mine = decay_coef * vel_v[:, cols(k)].astype(F32) + grad.astype(F32)
        vloc[k] = mine
        v_send[k] = mine.astype(BF16)
        if relay:
            v_first[k] = go(remote(v_send.at[k], v_hop.at[k], hop1))
        else:
            v_last[k] = go(remote(v_send.at[k], v_recv.at[k], hop2))

    def relay_velocity(k):
        if relay:
            v_first[k].wait_recv()
            v_last[k] = go(remote(v_hop.at[k], v_recv.at[k], hop2))

    for k in range(CHUNKS):
        dstream(k)
        gather_own(k)
        if k < AHEAD:
            gather_z(k)
    out_copies = [local(stream_v, stream_out)]
    for i in range(CHUNKS + 3):
        if i < CHUNKS:
            gather_y(i)
            if i + AHEAD < CHUNKS:
                gather_z(i + AHEAD)
            if (i + 1) % QUARTER == 0:
                point(4 + (i + 1) // QUARTER)
        if 0 <= i - 1 < CHUNKS:
            forward_y(i - 1)
        if 0 <= i - 3:
            send_velocity(i - 3)
            if i - 4 >= 0 and bit == 1:
                relay_velocity(i - 4)
        if 0 <= i - 2 < CHUNKS:
            weight_part(i - 2)
            attn_part(i - 2)
    ga_send[...] = (ga[:, GROUP:] * inv_width).astype(BF16).reshape(16, 32, GROUP)
    ga_swap = go(remote(ga_send, grad_attn_out.at[:, c], sibling))
    ga_own[...] = (ga[:, :GROUP] * inv_width).astype(BF16).reshape(16, 32, GROUP)
    out_copies.append(local(ga_own, grad_attn_out.at[:, c]))
    for k in range(CHUNKS - 1 if bit == 1 else 0, CHUNKS):
        relay_velocity(k)

    for copy in w_last:
        copy.wait_recv()
    for k in range(CHUNKS):
        v_last[k].wait_recv()
        mixed = 0.5 * (vloc[k] + v_recv[k].astype(F32))
        nv_v[:, cols(k)] = mixed.astype(BF16)
        mean = 0.5 * (wcat[:GROUP, cols(k)].astype(F32) + w_recv[:, cols(k)].astype(F32))
        nw_v[:, cols(k)] = (mean - rate[0] * mixed).astype(BF16)
        out_copies.append(local(nv_v.at[:, cols(k)], new_velocity_out.at[:, cols(k)]))
        out_copies.append(local(nw_v.at[:, cols(k)], new_weight_out.at[:, cols(k)]))
    ga_swap.wait_recv()
    for copy in out_copies:
        copy.wait()
    for copy in sends:
        copy.wait_send()


def step_with(bit, *operands):
    any_spec = pl.BlockSpec(memory_space=pl.ANY)
    vmem = lambda *shape: pltpu.VMEM(shape, BF16)
    wide = lambda *shape: pltpu.VMEM(shape, F32)
    remote_slots = 2 + 2 + CHUNKS * (2 + 2 + 3 + 3 + 8 + 2 + 1 + 2) + 1 + 2 * PIECES
    return pl.pallas_call(
        partial(kernel, bit),
        out_shape=(
            jax.ShapeDtypeStruct((32, D), BF16),
            jax.ShapeDtypeStruct((16, 2, 32, GROUP), BF16),
            jax.ShapeDtypeStruct((GROUP, D), BF16),
            jax.ShapeDtypeStruct((GROUP, D), BF16),
        ),
        in_specs=[any_spec] * 7 + [pl.BlockSpec(memory_space=pltpu.SMEM)],
        out_specs=(any_spec,) * 4,
        scratch_shapes=[
            vmem(16, 32, 2 * GROUP),
            vmem(2 * GROUP, D),
            vmem(2 * GROUP, 512),
            vmem(CHUNKS, 2, 2, 128, WIDE // 2),
            vmem(CHUNKS, 2, 2, 128, WIDE // 2),
            wide(CHUNKS, 2, 2, 128, WIDE // 2),
            vmem(CHUNKS, 2, 128, WIDE // 2),
            vmem(CHUNKS, 2, 128, WIDE // 2),
            vmem(CHUNKS, 4, 32, WIDE),
            vmem(CHUNKS, 3, 32, WIDE),
            vmem(CHUNKS, 16, 32, WIDE),
            vmem(32, D),
            vmem(16, 128),
            vmem(32, D),
            vmem(32, D),
            wide(32, D),
            vmem(32, D),
            vmem(GROUP, D),
            wide(512, 2 * GROUP),
            vmem(16, 32, GROUP),
            vmem(16, 32, GROUP),
            wide(CHUNKS, GROUP, WIDE),
            vmem(CHUNKS, GROUP, WIDE),
            vmem(CHUNKS, GROUP, WIDE),
            wide(CHUNKS, GROUP, WIDE),
            vmem(CHUNKS, GROUP, WIDE),
            vmem(CHUNKS, GROUP, WIDE),
            vmem(CHUNKS, GROUP, WIDE),
            vmem(GROUP, D),
            vmem(GROUP, D),
            vmem(GROUP, D),
            vmem(GROUP, D),
            pltpu.SemaphoreType.DMA((7 + 2 + 2 * CHUNKS,)),
            pltpu.SemaphoreType.DMA((remote_slots,)),
            pltpu.SemaphoreType.DMA((remote_slots,)),
        ],
        compiler_params=pltpu.CompilerParams(
            collective_id=bit, has_side_effects=True, vmem_limit_bytes=48 * 1024 * 1024
        ),
        cost_estimate=pl.CostEstimate(
            flops=6 * TOK * GROUP * D, bytes_accessed=8 * 1024 * 1024, transcendentals=64
        ),
        name="step_bit%d" % bit,
    )(*operands)


def per_device(
    attn_out, resid_in, out_weight, velocity, norm_gain, grad_normed, grad_resid, step_count
):
    peer_bit = step_count[0] % 4
    rate = plan_rate(step_count)
    stream, grad_attn, new_weight, new_velocity = lax.switch(
        peer_bit,
        [partial(step_with, bit) for bit in range(4)],
        attn_out.reshape(16, 2, 32, GROUP),
        resid_in[0],
        out_weight[0],
        velocity[0],
        norm_gain.reshape(16, 128),
        grad_normed[0],
        grad_resid[0],
        rate,
    )
    return (
        stream[None],
        grad_attn.reshape(1, TOK, GROUP),
        new_weight[None],
        new_velocity[None],
    )


def solution(mesh):
    rows = P("replica", "tensor", None)
    heads = P("replica", None, "tensor")
    return jax.shard_map(
        per_device,
        mesh=mesh,
        in_specs=(heads, rows, rows, rows, P(), rows, rows, P()),
        out_specs=(rows, heads, rows, rows),
        check_vma=False,
    )
```

```python
from functools import partial

import jax
import jax.numpy as jnp
from jax import lax
from jax.experimental import pallas as pl
from jax.experimental.pallas import tpu as pltpu
from jax.sharding import PartitionSpec as P

D = 2048
INNER = 4096
TOK = 1024
GROUP = 128
CHUNKS = 4
WIDE = D // CHUNKS
AHEAD = CHUNKS // 2
QUARTER = CHUNKS // 4
PIECES = 8
ONLY = ((0,) * 8, (0, 0, 1, 1, 2, 3, 5, 7))
FIRST = ((0,) * 8, (0, 0, 1, 1, 2, 2, 3, 3))
LAST = ((3,) * 8, (7, 7, 8, 8, 8, 8, 8, 8))
BF16 = jnp.bfloat16
F32 = jnp.float32
MESH = pl.DeviceIdType.MESH

norm_eps = 1e-05
decay_coef = 0.9
step_span = 1048576.0
inv_width = INNER ** (-0.5)


def plan_rate(step_value):
    phase = step_value.astype(jnp.float32) * (jnp.pi / step_span)
    return 0.02 + 0.04 * (1.0 + jnp.cos(phase))


def flip(digit, mask):
    if mask == 1:
        return digit + 1 - 2 * (digit % 2)
    if mask == 2:
        return (digit + 2) % 4
    return 3 - digit


def cols(k):
    return pl.ds(k * WIDE, WIDE)


def kernel(
    bit,
    attn, resid, weight, velocity, gain, grad_normed, grad_resid, rate,
    stream_out, grad_attn_out, new_weight_out, new_velocity_out,
    acat, wcat, acat_t, pcat, wp, keep, s2, r2, s3, r3, full,
    resid_v, gain_v, gn_v, gr_v, up_v, stream_v, vel_v,
    ga, ga_send, ga_own, g_own, g_send, g_recv, vloc, v_send, v_hop, v_recv, w_hop, w_recv,
    nw_v, nv_v, local_sem, send_sem, recv_sem,
):
    me_r = lax.axis_index("replica")
    me_t = lax.axis_index("tensor")
    y, z, c = me_t // 8, (me_t // 2) % 4, me_t % 2
    relay = bit % 2 == 1

    def at(y_, z_, c_):
        return (me_r, (y_ * 4 + z_) * 2 + c_)

    def peer_at(mask):
        if bit < 2:
            return (me_r - me_r % 4 + flip(me_r % 4, mask), me_t)
        return (flip(me_r // 4, mask) * 4 + me_r % 4, me_t)

    sibling = at(y, z, 1 - c)
    y1, y3 = at(flip(y, 1), z, c), at(flip(y, 3), z, c)
    z_at = [at(y, flip(z, j), c) for j in (1, 2, 3)]
    if relay:
        one, three = peer_at(1)[0], peer_at(3)[0]
        hop1 = (one * (1 - c) + three * c, me_t)
        hop2 = (three * (1 - c) + one * c, me_t)
        peers = [hop1, hop2]
    else:
        hop1 = hop2 = peer_at(1)
        peers = [hop2]

    slots = [0]

    def remote(src, dst, target):
        slot = slots[0]
        slots[0] += 1
        return pltpu.make_async_remote_copy(
            src_ref=src, dst_ref=dst, send_sem=send_sem.at[slot], recv_sem=recv_sem.at[slot],
            device_id=target, device_id_type=MESH,
        )

    local_slots = [0]

    def local(src, dst):
        slot = local_slots[0]
        local_slots[0] += 1
        copy = pltpu.make_async_copy(src, dst, local_sem.at[slot])
        copy.start()
        return copy

    barrier = pltpu.get_barrier_semaphore()
    across = {1: at(flip(y, 1), z, 1 - c), 3: at(flip(y, 3), z, 1 - c)}
    partners = [sibling, y1, y3, across[1], across[3]] + z_at + peers
    for partner in partners:
        pl.semaphore_signal(barrier, inc=1, device_id=partner, device_id_type=MESH)

    in_a = local(attn.at[:, c], acat.at[:, :, pl.ds(0, GROUP)])
    in_w = local(weight, wcat.at[pl.ds(0, GROUP)])
    in_rest = [
        local(resid, resid_v), local(gain, gain_v), local(grad_normed, gn_v),
        local(grad_resid, gr_v), local(velocity, vel_v),
    ]
    pl.semaphore_wait(barrier, len(partners))

    sends = []

    def go(copy):
        copy.start()
        sends.append(copy)
        return copy

    along_y = {1: y1, 3: y3}
    first, second = (1, 3), (3, 1)
    half = WIDE // 2

    def part(k, h):
        return pl.ds(k * WIDE + h * half, half)

    own_lanes, other_lanes = pl.ds(0, GROUP), pl.ds(GROUP, GROUP)
    attn_y, weight_y, weight_over = {}, {}, {}

    def send_attn(h):
        attn_y[h] = []
        for slot, mask in enumerate((first[h], 2)):
            dest = pl.ds(flip(y, mask) * 4, 4)
            for core, lanes, target in (
                (c, own_lanes, along_y[first[h]]), (1 - c, other_lanes, across[first[h]])
            ):
                there = pcat.at[h, slot, :, :, lanes]
                attn_y[h].append(go(remote(attn.at[dest, core], there, target)))

    def send_weight(k):
        for h in (0, 1):
            there = wp.at[k, h, own_lanes]
            weight_y[k, h] = go(remote(weight.at[:, part(k, h)], there, along_y[first[h]]))

    send_attn(0)
    send_attn(1)
    send_weight(0)
    sib_a = go(remote(attn.at[:, 1 - c], acat.at[:, :, pl.ds(GROUP, GROUP)], sibling))
    sib_w = go(remote(weight, wcat.at[pl.ds(GROUP, GROUP)], sibling))
    piece = GROUP // PIECES
    rows = [pl.ds(i * piece, piece) for i in range(PIECES)]
    for k in range(1, AHEAD):
        send_weight(k)
    w_first = [remote(weight.at[r], w_hop.at[r], hop1) for r in rows] if relay else []
    w_last = [
        remote((w_hop if relay else weight).at[r], w_recv.at[r], hop2) for r in rows
    ]
    sends.extend(w_first + w_last)

    def point(i):
        if relay:
            for n in range(PIECES):
                if i == FIRST[bit // 2][n]:
                    w_first[n].start()
                if i == LAST[bit // 2][n]:
                    w_first[n].wait_recv()
                    w_last[n].start()
        else:
            for n in range(PIECES):
                if i == ONLY[bit // 2][n]:
                    w_last[n].start()

    point(0)
    in_a.wait()
    in_w.wait()
    sib_a.wait_recv()
    sib_w.wait_recv()

    def rows_for(dest):
        return acat[pl.ds(dest * 4, 4)].reshape(128, 2 * GROUP)

    def product(dest, k, h):
        return (
            jnp.dot(rows_for(dest), wcat[:, part(k, h)], preferred_element_type=F32) * inv_width
        )

    step2, step3 = {}, {}

    def hold(k):
        for h in (0, 1):
            keep[k, h, 1] = product(flip(y, second[h]), k, h)
            keep[k, h, 0] = product(y, k, h)

    def fetch(k):
        for h in (0, 1):
            weight_y[k, h].wait_recv()
            here, there = wp.at[k, h, own_lanes], wp.at[k, h, other_lanes]
            weight_over[k, h] = go(remote(here, there, sibling))

    def send2(k):
        for h in (0, 1):
            if k == 0:
                for copy in attn_y[h]:
                    copy.wait_recv()
            weight_over[k, h].wait_recv()
            more = jnp.dot(
                pcat[h].reshape(256, 2 * GROUP), wp[k, h], preferred_element_type=F32
            ) * inv_width
            s2[k, h] = (keep[k, h, 1] + more[128:]).astype(BF16)
            step2[k, h] = go(remote(s2.at[k, h], r2.at[k, h], along_y[second[h]]))
            keep[k, h, 0] += more[:128]

    def send3(k):
        for h in (0, 1):
            step2[k, h].wait_recv()
            total = keep[k, h, 0] + r2[k, h].astype(F32)
            s3[k, :, :, pl.ds(h * half, half)] = total.astype(BF16).reshape(4, 32, half)
        step3[k] = [
            go(remote(s3.at[k, flip(z, j)], r3.at[k, j - 1], z_at[j - 1])) for j in (1, 2, 3)
        ]

    sums = [jnp.zeros((32, 1), F32), jnp.zeros((32, 1), F32)]

    def add_stream(k):
        projected = s3[k, z].astype(F32)
        for j in (1, 2, 3):
            step3[k][j - 1].wait_recv()
            projected += r3[k, j - 1].astype(F32)
        stream = (resid_v[:, cols(k)].astype(F32) + projected).astype(BF16)
        stream_v[:, cols(k)] = stream
        stream32 = stream.astype(F32)
        sums[0] += jnp.sum(stream32 * stream32, axis=-1, keepdims=True)
        sums[1] += jnp.sum(up_v[:, cols(k)] * stream32, axis=-1, keepdims=True)

    hold(0)
    hold(1)
    fetch(0)
    for k in range(CHUNKS):
        if k + AHEAD < CHUNKS:
            send_weight(k + AHEAD)
        if k + 1 < CHUNKS:
            fetch(k + 1)
        send2(k)
        if k + 2 < CHUNKS:
            hold(k + 2)
        if k >= 1:
            send3(k - 1)
        if k == 1:
            for copy in in_rest:
                copy.wait()
            gain32 = gain_v[...].astype(F32)
            for i in range(D // 128):
                lanes = pl.ds(i * 128, 128)
                up_v[:, lanes] = gain32[i : i + 1] * gn_v[:, lanes].astype(F32)
            acat_t[...] = acat[...].reshape(512, 2 * GROUP).T
        if k >= 2:
            add_stream(k - 2)
        if (k + 1) % QUARTER == 0:
            point((k + 1) // QUARTER)
    send3(CHUNKS - 1)
    add_stream(CHUNKS - 2)
    add_stream(CHUNKS - 1)
    squares, inner = sums
    inv_rms = lax.rsqrt(squares / D + norm_eps)
    factor = inv_rms * inv_rms * inv_rms * inner / D

    own = y * 4 + z
    gz, gy, gf = {}, {}, {}

    def dstream(k):
        d = (
            gr_v[:, cols(k)].astype(F32)
            + inv_rms * up_v[:, cols(k)]
            - stream_v[:, cols(k)].astype(F32) * factor
        )
        full[k, own] = d.astype(BF16)

    def gather_own(k):
        block = full.at[k, own]
        gy[k] = {m: [go(remote(block, block, along_y[m]))] for m in (1, 3)}

    def gather_z(k):
        block = full.at[k, own]
        gz[k] = [go(remote(block, block, z_at[j - 1])) for j in (1, 2, 3)]

    def gather_y(k):
        for j in (1, 2, 3):
            gz[k][j - 1].wait_recv()
            block = full.at[k, y * 4 + flip(z, j)]
            for m in (1, 3):
                gy[k][m].append(go(remote(block, block, along_y[m])))

    def forward_y(k):
        for h in (0, 1):
            for copy in gy[k][first[h]]:
                copy.wait_recv()
            block = full.at[k, pl.ds(flip(y, first[h]) * 4, 4), :, pl.ds(h * half, half)]
            gf[k, h] = go(remote(block, block, along_y[second[h]]))

    v_first, v_last, g_swap = {}, {}, {}

    def weight_part(k):
        gf[k, 0].wait_recv()
        gf[k, 1].wait_recv()
        rows = full[k].reshape(512, WIDE)
        both = jnp.dot(acat_t[...], rows, preferred_element_type=F32)
        g_send[k] = both[GROUP:].astype(BF16)
        g_own[k] = both[:GROUP]
        g_swap[k] = go(remote(g_send.at[k], g_recv.at[k], sibling))

    def attn_part(k):
        rows = full[k].reshape(512, WIDE)
        share = lax.dot_general(
            rows, wcat[:, cols(k)], (((1,), (1,)), ((), ())), preferred_element_type=F32
        )
        ga[...] = share if k == 0 else ga[...] + share

    def send_velocity(k):
        g_swap[k].wait_recv()
        grad = ((g_own[k] + g_recv[k].astype(F32)) * inv_width).astype(BF16)
        mine = decay_coef * vel_v[:, cols(k)].astype(F32) + grad.astype(F32)
        vloc[k] = mine
        v_send[k] = mine.astype(BF16)
        if relay:
            v_first[k] = go(remote(v_send.at[k], v_hop.at[k], hop1))
        else:
            v_last[k] = go(remote(v_send.at[k], v_recv.at[k], hop2))

    def relay_velocity(k):
        if relay:
            v_first[k].wait_recv()
            v_last[k] = go(remote(v_hop.at[k], v_recv.at[k], hop2))

    for k in range(CHUNKS):
        dstream(k)
        gather_own(k)
        if k < AHEAD:
            gather_z(k)
    out_copies = [local(stream_v, stream_out)]
    for i in range(CHUNKS + 3):
        if i < CHUNKS:
            gather_y(i)
            if i + AHEAD < CHUNKS:
                gather_z(i + AHEAD)
            if (i + 1) % QUARTER == 0:
                point(4 + (i + 1) // QUARTER)
        if 0 <= i - 1 < CHUNKS:
            forward_y(i - 1)
        if 0 <= i - 3:
            send_velocity(i - 3)
            if i - 4 >= 0 and bit == 1:
                relay_velocity(i - 4)
        if 0 <= i - 2 < CHUNKS:
            weight_part(i - 2)
            attn_part(i - 2)
    ga_send[...] = (ga[:, GROUP:] * inv_width).astype(BF16).reshape(16, 32, GROUP)
    ga_swap = go(remote(ga_send, grad_attn_out.at[:, c], sibling))
    ga_own[...] = (ga[:, :GROUP] * inv_width).astype(BF16).reshape(16, 32, GROUP)
    out_copies.append(local(ga_own, grad_attn_out.at[:, c]))
    for k in range(CHUNKS - 1 if bit == 1 else 0, CHUNKS):
        relay_velocity(k)

    for copy in w_last:
        copy.wait_recv()
    for k in range(CHUNKS):
        v_last[k].wait_recv()
        mixed = 0.5 * (vloc[k] + v_recv[k].astype(F32))
        nv_v[:, cols(k)] = mixed.astype(BF16)
        mean = 0.5 * (wcat[:GROUP, cols(k)].astype(F32) + w_recv[:, cols(k)].astype(F32))
        nw_v[:, cols(k)] = (mean - rate[0] * mixed).astype(BF16)
        out_copies.append(local(nv_v.at[:, cols(k)], new_velocity_out.at[:, cols(k)]))
        out_copies.append(local(nw_v.at[:, cols(k)], new_weight_out.at[:, cols(k)]))
    ga_swap.wait_recv()
    for copy in out_copies:
        copy.wait()
    for copy in sends:
        copy.wait_send()


def step_with(bit, *operands):
    any_spec = pl.BlockSpec(memory_space=pl.ANY)
    vmem = lambda *shape: pltpu.VMEM(shape, BF16)
    wide = lambda *shape: pltpu.VMEM(shape, F32)
    remote_slots = 2 + 2 + CHUNKS * (2 + 2 + 2 + 3 + 3 + 8 + 2 + 1 + 2) + 9 + 2 * PIECES
    return pl.pallas_call(
        partial(kernel, bit),
        out_shape=(
            jax.ShapeDtypeStruct((32, D), BF16),
            jax.ShapeDtypeStruct((16, 2, 32, GROUP), BF16),
            jax.ShapeDtypeStruct((GROUP, D), BF16),
            jax.ShapeDtypeStruct((GROUP, D), BF16),
        ),
        in_specs=[any_spec] * 7 + [pl.BlockSpec(memory_space=pltpu.SMEM)],
        out_specs=(any_spec,) * 4,
        scratch_shapes=[
            vmem(16, 32, 2 * GROUP),
            vmem(2 * GROUP, D),
            vmem(2 * GROUP, 512),
            vmem(2, 2, 4, 32, 2 * GROUP),
            vmem(CHUNKS, 2, 2 * GROUP, WIDE // 2),
            wide(CHUNKS, 2, 2, 128, WIDE // 2),
            vmem(CHUNKS, 2, 128, WIDE // 2),
            vmem(CHUNKS, 2, 128, WIDE // 2),
            vmem(CHUNKS, 4, 32, WIDE),
            vmem(CHUNKS, 3, 32, WIDE),
            vmem(CHUNKS, 16, 32, WIDE),
            vmem(32, D),
            vmem(16, 128),
            vmem(32, D),
            vmem(32, D),
            wide(32, D),
            vmem(32, D),
            vmem(GROUP, D),
            wide(512, 2 * GROUP),
            vmem(16, 32, GROUP),
            vmem(16, 32, GROUP),
            wide(CHUNKS, GROUP, WIDE),
            vmem(CHUNKS, GROUP, WIDE),
            vmem(CHUNKS, GROUP, WIDE),
            wide(CHUNKS, GROUP, WIDE),
            vmem(CHUNKS, GROUP, WIDE),
            vmem(CHUNKS, GROUP, WIDE),
            vmem(CHUNKS, GROUP, WIDE),
            vmem(GROUP, D),
            vmem(GROUP, D),
            vmem(GROUP, D),
            vmem(GROUP, D),
            pltpu.SemaphoreType.DMA((7 + 2 + 2 * CHUNKS,)),
            pltpu.SemaphoreType.DMA((remote_slots,)),
            pltpu.SemaphoreType.DMA((remote_slots,)),
        ],
        compiler_params=pltpu.CompilerParams(
            collective_id=bit, has_side_effects=True, vmem_limit_bytes=48 * 1024 * 1024
        ),
        cost_estimate=pl.CostEstimate(
            flops=6 * TOK * GROUP * D, bytes_accessed=8 * 1024 * 1024, transcendentals=64
        ),
        name="step_bit%d" % bit,
    )(*operands)


def per_device(
    attn_out, resid_in, out_weight, velocity, norm_gain, grad_normed, grad_resid, step_count
):
    peer_bit = step_count[0] % 4
    rate = plan_rate(step_count)
    stream, grad_attn, new_weight, new_velocity = lax.switch(
        peer_bit,
        [partial(step_with, bit) for bit in range(4)],
        attn_out.reshape(16, 2, 32, GROUP),
        resid_in[0],
        out_weight[0],
        velocity[0],
        norm_gain.reshape(16, 128),
        grad_normed[0],
        grad_resid[0],
        rate,
    )
    return (
        stream[None],
        grad_attn.reshape(1, TOK, GROUP),
        new_weight[None],
        new_velocity[None],
    )


def solution(mesh):
    rows = P("replica", "tensor", None)
    heads = P("replica", None, "tensor")
    return jax.shard_map(
        per_device,
        mesh=mesh,
        in_specs=(heads, rows, rows, rows, P(), rows, rows, P()),
        out_specs=(rows, heads, rows, rows),
        check_vma=False,
    )
```

```python
from functools import partial

import jax
import jax.numpy as jnp
from jax import lax
from jax.experimental import pallas as pl
from jax.experimental.pallas import tpu as pltpu
from jax.sharding import PartitionSpec as P

D = 2048
INNER = 4096
TOK = 1024
GROUP = 128
CHUNKS = 4
WIDE = D // CHUNKS
AHEAD = CHUNKS // 2
QUARTER = CHUNKS // 4
PIECES = 8
ONLY = ((0,) * 8, (0, 0, 1, 1, 2, 2, 5, 6))
FIRST = ((0,) * 8, (0, 0, 1, 1, 2, 2, 3, 3))
LAST = ((3,) * 8, (7, 7, 8, 8, 8, 8, 8, 8))
BF16 = jnp.bfloat16
F32 = jnp.float32
MESH = pl.DeviceIdType.MESH

norm_eps = 1e-05
decay_coef = 0.9
step_span = 1048576.0
inv_width = INNER ** (-0.5)


def plan_rate(step_value):
    phase = step_value.astype(jnp.float32) * (jnp.pi / step_span)
    return 0.02 + 0.04 * (1.0 + jnp.cos(phase))


def flip(digit, mask):
    if mask == 1:
        return digit + 1 - 2 * (digit % 2)
    if mask == 2:
        return (digit + 2) % 4
    return 3 - digit


def cols(k):
    return pl.ds(k * WIDE, WIDE)


def kernel(
    bit,
    attn, resid, weight, velocity, gain, grad_normed, grad_resid, rate,
    stream_out, grad_attn_out, new_weight_out, new_velocity_out,
    acat, wcat, acat_t, pcat, wp, keep, s2, r2, s3, r3, full,
    resid_v, gain_v, gn_v, gr_v, up_v, vel_v,
    ga, ga_send, g_own, g_send, g_recv, vloc, v_send, v_hop, v_recv, w_hop, w_recv,
    local_sem, send_sem, recv_sem,
):
    me_r = lax.axis_index("replica")
    me_t = lax.axis_index("tensor")
    y, z, c = me_t // 8, (me_t // 2) % 4, me_t % 2
    relay = bit % 2 == 1

    def at(y_, z_, c_):
        return (me_r, (y_ * 4 + z_) * 2 + c_)

    def peer_at(mask):
        if bit < 2:
            return (me_r - me_r % 4 + flip(me_r % 4, mask), me_t)
        return (flip(me_r // 4, mask) * 4 + me_r % 4, me_t)

    sibling = at(y, z, 1 - c)
    y1, y3 = at(flip(y, 1), z, c), at(flip(y, 3), z, c)
    z_at = [at(y, flip(z, j), c) for j in (1, 2, 3)]
    if relay:
        one, three = peer_at(1)[0], peer_at(3)[0]
        hop1 = (one * (1 - c) + three * c, me_t)
        hop2 = (three * (1 - c) + one * c, me_t)
        peers = [hop1, hop2]
    else:
        hop1 = hop2 = peer_at(1)
        peers = [hop2]

    slots = [0]

    def remote(src, dst, target):
        slot = slots[0]
        slots[0] += 1
        return pltpu.make_async_remote_copy(
            src_ref=src, dst_ref=dst, send_sem=send_sem.at[slot], recv_sem=recv_sem.at[slot],
            device_id=target, device_id_type=MESH,
        )

    local_slots = [0]

    def local(src, dst):
        slot = local_slots[0]
        local_slots[0] += 1
        copy = pltpu.make_async_copy(src, dst, local_sem.at[slot])
        copy.start()
        return copy

    barrier = pltpu.get_barrier_semaphore()
    across = {1: at(flip(y, 1), z, 1 - c), 3: at(flip(y, 3), z, 1 - c)}
    partners = [sibling, y1, y3, across[1], across[3]] + z_at + peers
    for partner in partners:
        pl.semaphore_signal(barrier, inc=1, device_id=partner, device_id_type=MESH)

    in_a = local(attn.at[:, c], acat.at[:, :, pl.ds(0, GROUP)])
    in_w = local(weight, wcat.at[pl.ds(0, GROUP)])
    in_rest = [
        local(resid, resid_v), local(gain, gain_v), local(grad_normed, gn_v),
        local(grad_resid, gr_v), local(velocity, vel_v),
    ]
    pl.semaphore_wait(barrier, len(partners))

    sends = []

    def go(copy):
        copy.start()
        sends.append(copy)
        return copy

    along_y = {1: y1, 3: y3}
    first, second = (1, 3), (3, 1)
    half = WIDE // 2

    def part(k, h):
        return pl.ds(k * WIDE + h * half, half)

    own_lanes, other_lanes = pl.ds(0, GROUP), pl.ds(GROUP, GROUP)
    attn_y, weight_y, weight_over = {}, {}, {}

    def send_attn(h):
        attn_y[h] = []
        for slot, mask in enumerate((first[h], 2)):
            dest = pl.ds(flip(y, mask) * 4, 4)
            for core, lanes, target in (
                (c, own_lanes, along_y[first[h]]), (1 - c, other_lanes, across[first[h]])
            ):
                there = pcat.at[h, slot, :, :, lanes]
                attn_y[h].append(go(remote(attn.at[dest, core], there, target)))

    def send_weight(k):
        for h in (0, 1):
            there = wp.at[k, h, own_lanes]
            weight_y[k, h] = go(remote(weight.at[:, part(k, h)], there, along_y[first[h]]))

    send_attn(0)
    send_attn(1)
    send_weight(0)
    sib_a = go(remote(attn.at[:, 1 - c], acat.at[:, :, pl.ds(GROUP, GROUP)], sibling))
    sib_w = go(remote(weight, wcat.at[pl.ds(GROUP, GROUP)], sibling))
    piece = GROUP // PIECES
    rows = [pl.ds(i * piece, piece) for i in range(PIECES)]
    for k in range(1, AHEAD):
        send_weight(k)
    w_first = [remote(weight.at[r], w_hop.at[r], hop1) for r in rows] if relay else []
    w_last = [
        remote((w_hop if relay else weight).at[r], w_recv.at[r], hop2) for r in rows
    ]
    sends.extend(w_first + w_last)

    def point(i):
        if relay:
            for n in range(PIECES):
                if i == FIRST[bit // 2][n]:
                    w_first[n].start()
                if i == LAST[bit // 2][n]:
                    w_first[n].wait_recv()
                    w_last[n].start()
        else:
            for n in range(PIECES):
                if i == ONLY[bit // 2][n]:
                    w_last[n].start()

    point(0)
    in_a.wait()
    in_w.wait()
    sib_a.wait_recv()
    sib_w.wait_recv()

    def rows_for(dest):
        return acat[pl.ds(dest * 4, 4)].reshape(128, 2 * GROUP)

    def product(dest, k, h):
        return (
            jnp.dot(rows_for(dest), wcat[:, part(k, h)], preferred_element_type=F32) * inv_width
        )

    step2, step3 = {}, {}

    def hold(k):
        for h in (0, 1):
            keep[k, h, 1] = product(flip(y, second[h]), k, h)
            keep[k, h, 0] = product(y, k, h)

    def fetch(k):
        for h in (0, 1):
            weight_y[k, h].wait_recv()
            here, there = wp.at[k, h, own_lanes], wp.at[k, h, other_lanes]
            weight_over[k, h] = go(remote(here, there, sibling))

    def send2(k):
        for h in (0, 1):
            if k == 0:
                for copy in attn_y[h]:
                    copy.wait_recv()
            weight_over[k, h].wait_recv()
            more = jnp.dot(
                pcat[h].reshape(256, 2 * GROUP), wp[k, h], preferred_element_type=F32
            ) * inv_width
            s2[k, h] = (keep[k, h, 1] + more[128:]).astype(BF16)
            step2[k, h] = go(remote(s2.at[k, h], r2.at[k, h], along_y[second[h]]))
            keep[k, h, 0] += more[:128]

    def send3(k):
        for h in (0, 1):
            step2[k, h].wait_recv()
            total = keep[k, h, 0] + r2[k, h].astype(F32)
            s3[k, :, :, pl.ds(h * half, half)] = total.astype(BF16).reshape(4, 32, half)
        step3[k] = [
            go(remote(s3.at[k, flip(z, j)], r3.at[k, j - 1], z_at[j - 1])) for j in (1, 2, 3)
        ]

    sums = [jnp.zeros((32, 1), F32), jnp.zeros((32, 1), F32)]

    def add_stream(k):
        projected = s3[k, z].astype(F32)
        for j in (1, 2, 3):
            step3[k][j - 1].wait_recv()
            projected += r3[k, j - 1].astype(F32)
        stream = (resid_v[:, cols(k)].astype(F32) + projected).astype(BF16)
        stream_out[:, cols(k)] = stream
        stream32 = stream.astype(F32)
        sums[0] += jnp.sum(stream32 * stream32, axis=-1, keepdims=True)
        sums[1] += jnp.sum(up_v[:, cols(k)] * stream32, axis=-1, keepdims=True)

    hold(0)
    hold(1)
    fetch(0)
    for k in range(CHUNKS):
        if k + AHEAD < CHUNKS:
            send_weight(k + AHEAD)
        if k + 1 < CHUNKS:
            fetch(k + 1)
        send2(k)
        if k + 2 < CHUNKS:
            hold(k + 2)
        if k >= 1:
            send3(k - 1)
        if k == 1:
            for copy in in_rest:
                copy.wait()
            gain32 = gain_v[...].astype(F32)
            for i in range(D // 128):
                lanes = pl.ds(i * 128, 128)
                up_v[:, lanes] = gain32[i : i + 1] * gn_v[:, lanes].astype(F32)
            acat_t[...] = acat[...].reshape(512, 2 * GROUP).T
        if k >= 2:
            add_stream(k - 2)
        if (k + 1) % QUARTER == 0:
            point((k + 1) // QUARTER)
    send3(CHUNKS - 1)
    add_stream(CHUNKS - 2)
    add_stream(CHUNKS - 1)
    squares, inner = sums
    inv_rms = lax.rsqrt(squares / D + norm_eps)
    factor = inv_rms * inv_rms * inv_rms * inner / D

    own = y * 4 + z
    gz, gy, gf = {}, {}, {}

    def dstream(k):
        d = (
            gr_v[:, cols(k)].astype(F32)
            + inv_rms * up_v[:, cols(k)]
            - stream_out[:, cols(k)].astype(F32) * factor
        )
        full[k, own] = d.astype(BF16)

    def gather_own(k):
        block = full.at[k, own]
        gy[k] = {m: [go(remote(block, block, along_y[m]))] for m in (1, 3)}

    def gather_z(k):
        block = full.at[k, own]
        gz[k] = [go(remote(block, block, z_at[j - 1])) for j in (1, 2, 3)]

    def gather_y(k):
        for j in (1, 2, 3):
            gz[k][j - 1].wait_recv()
            block = full.at[k, y * 4 + flip(z, j)]
            for m in (1, 3):
                gy[k][m].append(go(remote(block, block, along_y[m])))

    def forward_y(k):
        for h in (0, 1):
            for copy in gy[k][first[h]]:
                copy.wait_recv()
            block = full.at[k, pl.ds(flip(y, first[h]) * 4, 4), :, pl.ds(h * half, half)]
            gf[k, h] = go(remote(block, block, along_y[second[h]]))

    v_first, v_last, g_swap = {}, {}, {}

    def weight_part(k):
        gf[k, 0].wait_recv()
        gf[k, 1].wait_recv()
        rows = full[k].reshape(512, WIDE)
        both = jnp.dot(acat_t[...], rows, preferred_element_type=F32)
        g_send[k] = both[GROUP:].astype(BF16)
        g_own[k] = both[:GROUP]
        g_swap[k] = go(remote(g_send.at[k], g_recv.at[k], sibling))

    def attn_part(k):
        rows = full[k].reshape(512, WIDE)
        share = lax.dot_general(
            rows, wcat[:, cols(k)], (((1,), (1,)), ((), ())), preferred_element_type=F32
        )
        ga[...] = share if k == 0 else ga[...] + share

    def send_velocity(k):
        g_swap[k].wait_recv()
        grad = ((g_own[k] + g_recv[k].astype(F32)) * inv_width).astype(BF16)
        mine = decay_coef * vel_v[:, cols(k)].astype(F32) + grad.astype(F32)
        vloc[k] = mine
        v_send[k] = mine.astype(BF16)
        if relay:
            v_first[k] = go(remote(v_send.at[k], v_hop.at[k], hop1))
        else:
            v_last[k] = go(remote(v_send.at[k], v_recv.at[k], hop2))

    def relay_velocity(k):
        if relay:
            v_first[k].wait_recv()
            v_last[k] = go(remote(v_hop.at[k], v_recv.at[k], hop2))

    for k in range(CHUNKS):
        dstream(k)
        gather_own(k)
        if k < AHEAD:
            gather_z(k)
    for i in range(CHUNKS + 3):
        if i < CHUNKS:
            gather_y(i)
            if i + AHEAD < CHUNKS:
                gather_z(i + AHEAD)
            if (i + 1) % QUARTER == 0:
                point(4 + (i + 1) // QUARTER)
        if 0 <= i - 1 < CHUNKS:
            forward_y(i - 1)
        if 0 <= i - 3:
            send_velocity(i - 3)
            if i - 4 >= 0 and bit == 1:
                relay_velocity(i - 4)
        if 0 <= i - 2 < CHUNKS:
            weight_part(i - 2)
            attn_part(i - 2)
    ga_send[...] = (ga[:, GROUP:] * inv_width).astype(BF16).reshape(16, 32, GROUP)
    ga_swap = go(remote(ga_send, grad_attn_out.at[:, c], sibling))
    grad_attn_out[:, c] = (ga[:, :GROUP] * inv_width).astype(BF16).reshape(16, 32, GROUP)
    for k in range(CHUNKS - 1 if bit == 1 else 0, CHUNKS):
        relay_velocity(k)

    for copy in w_last:
        copy.wait_recv()
    for k in range(CHUNKS):
        v_last[k].wait_recv()
        mixed = 0.5 * (vloc[k] + v_recv[k].astype(F32))
        new_velocity_out[:, cols(k)] = mixed.astype(BF16)
        mean = 0.5 * (wcat[:GROUP, cols(k)].astype(F32) + w_recv[:, cols(k)].astype(F32))
        new_weight_out[:, cols(k)] = (mean - rate[0] * mixed).astype(BF16)
    ga_swap.wait_recv()
    for copy in sends:
        copy.wait_send()


def step_with(bit, *operands):
    any_spec = pl.BlockSpec(memory_space=pl.ANY)
    vmem = lambda *shape: pltpu.VMEM(shape, BF16)
    wide = lambda *shape: pltpu.VMEM(shape, F32)
    remote_slots = 2 + 2 + CHUNKS * (2 + 2 + 2 + 3 + 3 + 8 + 2 + 1 + 2) + 9 + 2 * PIECES
    return pl.pallas_call(
        partial(kernel, bit),
        out_shape=(
            jax.ShapeDtypeStruct((32, D), BF16),
            jax.ShapeDtypeStruct((16, 2, 32, GROUP), BF16),
            jax.ShapeDtypeStruct((GROUP, D), BF16),
            jax.ShapeDtypeStruct((GROUP, D), BF16),
        ),
        in_specs=[any_spec] * 7 + [pl.BlockSpec(memory_space=pltpu.SMEM)],
        out_specs=(pl.BlockSpec(memory_space=pltpu.VMEM),) * 4,
        scratch_shapes=[
            vmem(16, 32, 2 * GROUP),
            vmem(2 * GROUP, D),
            vmem(2 * GROUP, 512),
            vmem(2, 2, 4, 32, 2 * GROUP),
            vmem(CHUNKS, 2, 2 * GROUP, WIDE // 2),
            wide(CHUNKS, 2, 2, 128, WIDE // 2),
            vmem(CHUNKS, 2, 128, WIDE // 2),
            vmem(CHUNKS, 2, 128, WIDE // 2),
            vmem(CHUNKS, 4, 32, WIDE),
            vmem(CHUNKS, 3, 32, WIDE),
            vmem(CHUNKS, 16, 32, WIDE),
            vmem(32, D),
            vmem(16, 128),
            vmem(32, D),
            vmem(32, D),
            wide(32, D),
            vmem(GROUP, D),
            wide(512, 2 * GROUP),
            vmem(16, 32, GROUP),
            wide(CHUNKS, GROUP, WIDE),
            vmem(CHUNKS, GROUP, WIDE),
            vmem(CHUNKS, GROUP, WIDE),
            wide(CHUNKS, GROUP, WIDE),
            vmem(CHUNKS, GROUP, WIDE),
            vmem(CHUNKS, GROUP, WIDE),
            vmem(CHUNKS, GROUP, WIDE),
            vmem(GROUP, D),
            vmem(GROUP, D),
            pltpu.SemaphoreType.DMA((7,)),
            pltpu.SemaphoreType.DMA((remote_slots,)),
            pltpu.SemaphoreType.DMA((remote_slots,)),
        ],
        compiler_params=pltpu.CompilerParams(
            collective_id=bit, has_side_effects=True, vmem_limit_bytes=48 * 1024 * 1024
        ),
        cost_estimate=pl.CostEstimate(
            flops=6 * TOK * GROUP * D, bytes_accessed=8 * 1024 * 1024, transcendentals=64
        ),
        name="step_bit%d" % bit,
    )(*operands)


def per_device(
    attn_out, resid_in, out_weight, velocity, norm_gain, grad_normed, grad_resid, step_count
):
    peer_bit = step_count[0] % 4
    rate = plan_rate(step_count)
    stream, grad_attn, new_weight, new_velocity = lax.switch(
        peer_bit,
        [partial(step_with, bit) for bit in range(4)],
        attn_out.reshape(16, 2, 32, GROUP),
        resid_in[0],
        out_weight[0],
        velocity[0],
        norm_gain.reshape(16, 128),
        grad_normed[0],
        grad_resid[0],
        rate,
    )
    return (
        stream[None],
        grad_attn.reshape(1, TOK, GROUP),
        new_weight[None],
        new_velocity[None],
    )


def solution(mesh):
    rows = P("replica", "tensor", None)
    heads = P("replica", None, "tensor")
    return jax.shard_map(
        per_device,
        mesh=mesh,
        in_specs=(heads, rows, rows, rows, P(), rows, rows, P()),
        out_specs=(rows, heads, rows, rows),
        check_vma=False,
    )
```
